32 devices in a mesh: groups: 2 (over x), wide: 16 (over z, y, core).
Axes of the slice: x: 2, y: 2, z: 4, core: 2. Of those that a mesh axis runs over, the one named last changes fastest.
Arguments:
- queries: bfloat16 [64, 8192], P(('groups', 'wide')), parts along dimension 0, may hold values from -120 to 120
- key_cache_array: bfloat16 [64, 256, 512], P(('groups', 'wide')), parts along dimension 0, may hold values from -6.1 to 6.1
- value_cache_array: bfloat16 [64, 256, 512], P(('groups', 'wide')), parts along dimension 0, may hold values from -16 to 16
- fresh_keys: bfloat16 [64, 512], P(('groups', 'wide')), parts along dimension 0, may hold values from -6 to 6
- fresh_values: bfloat16 [64, 512], P(('groups', 'wide')), parts along dimension 0, may hold values from -16 to 16
- lengths: int32 [64], P(('groups', 'wide')), parts along dimension 0, may hold values from 1 to 256, 4096 in all
- resid: bfloat16 [64, 8192], P(('groups', 'wide')), parts along dimension 0, may hold values from -1.5 to 1.5
- gain: bfloat16 [8192], replicated, may hold values from 0.099609375 to 1.8984375
- gate_weight: bfloat16 [8192, 26624], P(None, 'wide'), may hold values from -0.0625 to 0.0625
- up_weight: bfloat16 [8192, 26624], P(None, 'wide'), may hold values from -0.0625 to 0.0625
- down_weight: bfloat16 [26624, 8192], P('wide'), may hold values from -0.0390625 to 0.0390625
Outputs:
- mixed: bfloat16 [64, 8192], P(('groups', 'wide')), parts along dimension 0
The draws below stay inside these ranges and needn't reach their ends.
There are 2 independent parts, one for each index of `groups`. The reference program is written for one: setup_inputs(seed, part) draws one part's arguments, and reference() takes and returns one part's arrays. A program takes and returns all parts, laid end to end along the dimension named above; an argument that names none is the same for every part. Nothing has to cross between parts.
All inputs are finite; a program needn't handle non-finite values. No bound on the sum of `lengths` on one device may be relied on, other than what follows from the above.
Results may differ from the reference program's by a relative error of at most 0.0055.
Values may be sent and summed in bfloat16 or wider, within the bound.
A program may use at most 192 MiB of HBM per device.

```python
import math
import jax
import jax.numpy as jnp
import numpy as np
from jax import lax

QUERY_HEADS = 64
KEY_VALUE_HEADS = 4
HEAD_SIZE = 128
FF_WIN = 26624
CACHE_LENGTH = 256
D_WIN = 8192
BATCH_ROWS = 32


def cache_normal(key):
    return jnp.clip(jax.random.normal(key, (BATCH_ROWS, CACHE_LENGTH, KEY_VALUE_HEADS * HEAD_SIZE), jnp.float32), -6.0, 6.0)


def draw_key_cache_array(key, part):
    shared_heads = cache_normal(key)
    return shared_heads.astype(jnp.bfloat16)


def draw_queries(key, part):
    key = jax.random.fold_in(key, 23)
    key_drawn = jax.random.fold_in(key, 0)
    drawn = jnp.clip(jax.random.normal(key_drawn, (BATCH_ROWS, QUERY_HEADS * HEAD_SIZE), jnp.float32), -6.0, 6.0)
    return drawn.astype(jnp.bfloat16)


def steps_of(key, shape, cuts, least, top_value):
    def one(position, shards_of):
        steps = jax.random.uniform(jax.random.fold_in(jax.random.fold_in(key, 6), position), (shards_of,), jnp.float32, least / len(cuts), top_value / len(cuts))
        return jnp.repeat(jnp.exp(steps), shape[position] // shards_of).reshape((-1,) + (1,) * (len(shape) - position - 1))

    factor_of = one(*cuts[0])
    for cut in cuts[1:]:
        factor_of = factor_of * one(*cut)
    return factor_of


def profile(number_of, total, reach, slope):
    weights = [(1 << 20) // math.isqrt(standing ** slope) + 1 for standing in range(2, number_of + 1)]
    spare, given = total - reach - (number_of - 1), [1] * (number_of - 1)
    while spare > 0:
        free = [i for i in range(number_of - 1) if given[i] < reach]
        pool, remaining = sum([weights[i] for i in free]), spare
        for i in free:
            extra = min(reach - given[i], max(1, remaining * weights[i] // pool), spare)
            given[i] = given[i] + extra
            spare = spare - extra
    return np.array([reach] + given)


def ragged(rng, amount, total, bound, skew):
    if amount == 2:
        one = jax.random.randint(rng, (), max(1, total - bound), min(bound, total - 1) + 1)
        return jnp.stack([one, total - one])
    tallies = jnp.asarray(profile(amount, total, bound, skew), jnp.int32)
    twos = (amount - 1) // 2
    giver, taker = tallies[1:1 + 2 * twos:2], tallies[2:2 + 2 * twos:2]
    slack = jnp.minimum(giver - 1, bound - taker)
    moved = jax.random.randint(jax.random.fold_in(rng, 1), (twos,), 0, 1 << 20) % (slack + 1)
    tallies = tallies.at[1:1 + 2 * twos:2].set(giver - moved).at[2:2 + 2 * twos:2].set(taker + moved)
    return tallies[jax.random.permutation(jax.random.fold_in(rng, 2), amount)]


def gaussian(stream_key, extent, scale, reach, cuts=(), kind=jnp.bfloat16):
    result = scale * jax.random.normal(stream_key, extent, jnp.float32)
    if cuts:
        result = result * steps_of(stream_key, extent, cuts, -0.22, 0.18)
    return jnp.clip(result, -reach, reach).astype(kind)


def setup_inputs(seed: int = 0, part: int = 0) -> dict:
    seeds = jax.random.split(jax.random.key(seed), 12)
    part_keys = jax.random.split(jax.random.fold_in(seeds[11], part), 12)
    queries = draw_queries(jax.random.fold_in(jax.random.fold_in(seeds[11], part), 71), part)
    key_cache_array = draw_key_cache_array(jax.random.fold_in(jax.random.fold_in(seeds[11], part), 71), part)
    value_cache_array = gaussian(part_keys[2], (BATCH_ROWS, CACHE_LENGTH, KEY_VALUE_HEADS * HEAD_SIZE), 4.0, 16.0, ((0, 16),))
    fresh_keys = gaussian(part_keys[3], (BATCH_ROWS, KEY_VALUE_HEADS * HEAD_SIZE), 1.0, 6.0, ((0, 16),))
    fresh_values = gaussian(part_keys[4], (BATCH_ROWS, KEY_VALUE_HEADS * HEAD_SIZE), 4.0, 16.0, ((0, 16),))
    lengths = ragged(part_keys[5], BATCH_ROWS, BATCH_ROWS * CACHE_LENGTH // 2, CACHE_LENGTH, 2).astype(jnp.int32)
    resid = gaussian(part_keys[6], (BATCH_ROWS, D_WIN), 0.25, 1.5, ((0, 16),))
    gain = jnp.clip(1.0 + 0.18 * jax.random.normal(seeds[7], (D_WIN,), jnp.float32), 0.099609375, 1.8984375).astype(jnp.bfloat16)
    gate_weight = gaussian(seeds[8], (D_WIN, FF_WIN), D_WIN ** -0.5, 0.0625, ((1, 16),))
    up_weight = gaussian(seeds[9], (D_WIN, FF_WIN), D_WIN ** -0.5, 0.0625, ((1, 16),))
    down_weight = gaussian(seeds[10], (FF_WIN, D_WIN), FF_WIN ** -0.5, 0.0390625, ((0, 16),))
    return dict(queries=queries, key_cache_array=key_cache_array, value_cache_array=value_cache_array, fresh_keys=fresh_keys, fresh_values=fresh_values, lengths=lengths, resid=resid, gain=gain, gate_weight=gate_weight, up_weight=up_weight, down_weight=down_weight)


NEG_FILL = -1e+30

def reference(queries, key_cache_array, value_cache_array, fresh_keys, fresh_values, lengths, resid, gain, gate_weight, up_weight, down_weight):
    queries_per_group = QUERY_HEADS // KEY_VALUE_HEADS
    score_scale = 1.0 / math.sqrt(HEAD_SIZE)
    query_vector = queries.astype(jnp.float32).reshape(BATCH_ROWS, KEY_VALUE_HEADS, queries_per_group, HEAD_SIZE)
    cached_key_rows = key_cache_array.astype(jnp.float32).reshape(BATCH_ROWS, CACHE_LENGTH, KEY_VALUE_HEADS, HEAD_SIZE)
    cached_value_rows = value_cache_array.astype(jnp.float32).reshape(BATCH_ROWS, CACHE_LENGTH, KEY_VALUE_HEADS, HEAD_SIZE)
    token_key = fresh_keys.astype(jnp.float32).reshape(BATCH_ROWS, KEY_VALUE_HEADS, HEAD_SIZE)
    token_value = fresh_values.astype(jnp.float32).reshape(BATCH_ROWS, KEY_VALUE_HEADS, HEAD_SIZE)
    scores = jnp.einsum('rhgd,rlhd->rhgl', query_vector, cached_key_rows) * score_scale
    own_score = jnp.einsum('rhgd,rhd->rhg', query_vector, token_key) * score_scale
    inside = (jnp.arange(CACHE_LENGTH, dtype=jnp.int32)[None, :] < lengths.astype(jnp.int32)[:, None])[:, None, None, :]
    scores = jnp.where(inside, scores, NEG_FILL)
    row_max = jnp.maximum(lax.optimization_barrier(jnp.max(scores, axis=-1)), own_score)
    weights = jnp.where(inside, jnp.exp(scores - row_max[..., None]), 0.0)
    own_weight = jnp.exp(own_score - row_max)
    totals = lax.optimization_barrier(jnp.sum(weights, axis=-1)) + own_weight
    weights_low = lax.optimization_barrier(weights.astype(jnp.bfloat16)).astype(jnp.float32)
    own_low = lax.optimization_barrier(own_weight.astype(jnp.bfloat16)).astype(jnp.float32)
    heads_out = jnp.einsum('rhgl,rlhd->rhgd', weights_low, cached_value_rows) + own_low[..., None] * token_value[:, :, None, :]
    attended = (heads_out / totals[..., None]).reshape(BATCH_ROWS, QUERY_HEADS * HEAD_SIZE)
    stream = resid.astype(jnp.float32) + attended
    normed = (stream * lax.rsqrt(lax.optimization_barrier(jnp.mean(stream * stream, axis=-1, keepdims=True)) + 1e-05) * gain.astype(jnp.float32)).astype(jnp.bfloat16)
    gate = jnp.dot(normed, gate_weight, preferred_element_type=jnp.float32)
    up_part = jnp.dot(normed, up_weight, preferred_element_type=jnp.float32)
    hidden = (jax.nn.silu(gate) * up_part).astype(jnp.bfloat16)
    down_part = jnp.dot(hidden, down_weight, preferred_element_type=jnp.float32)
    return (stream + down_part).astype(jnp.bfloat16)
```

```python
import functools
import math

import jax
import jax.numpy as jnp
from jax import lax
from jax.experimental import pallas as pl
from jax.experimental.pallas import tpu as pltpu
from jax.sharding import PartitionSpec as P

HEAD_SIZE = 128
NEG_FILL = -1e30
MESH = pl.DeviceIdType.MESH
MIB = 1024 * 1024

CHUNK = 512
GATHER_PIECES = 4
SUM_PIECES = 4


def kernel(
    n,
    gather_pieces,
    sum_pieces,
    lengths,
    queries,
    keys,
    values,
    fresh_keys,
    fresh_values,
    resid,
    gain,
    gate_w,
    up_w,
    down_w,
    out,
    q_in,
    k_in,
    v_in,
    fk_in,
    fv_in,
    r_in,
    g_in,
    q_heads,
    stream,
    gate_buf,
    up_buf,
    down_buf,
    gathered,
    gate_acc,
    up_acc,
    hidden,
    part32,
    part16,
    from_pair,
    to_chips,
    from_chips,
    in_sem,
    gate_sem,
    up_sem,
    down_sem,
    ag_send,
    ag_recv,
    fw_send,
    fw_recv,
    pair_send,
    pair_recv,
    rs_send,
    rs_recv,
):
    rows, width = queries.shape
    heads = width // HEAD_SIZE
    kv_heads = keys.shape[2] // HEAD_SIZE
    per_kv = heads // kv_heads
    length = keys.shape[1]
    chips = n // 2
    chunks = width // CHUNK
    gu_slots = gate_buf.shape[0]
    dn_slots = down_buf.shape[0]
    per_gather = chunks // gather_pieces
    per_sum = chunks // sum_pieces
    half = rows * chips

    me = lax.axis_index("wide")
    chip = me // 2
    core = lax.rem(me, 2)
    pair = me + 1 - 2 * core

    def gate_copy(t):
        slot = lax.rem(t, gu_slots)
        src = gate_w.at[pl.ds(pl.multiple_of(t * CHUNK, CHUNK), CHUNK)]
        return pltpu.make_async_copy(src, gate_buf.at[slot], gate_sem.at[slot])

    def up_copy(t):
        slot = lax.rem(t, gu_slots)
        src = up_w.at[pl.ds(pl.multiple_of(t * CHUNK, CHUNK), CHUNK)]
        return pltpu.make_async_copy(src, up_buf.at[slot], up_sem.at[slot])

    def down_copy(t):
        slot = lax.rem(t, dn_slots)
        src = down_w.at[:, pl.ds(pl.multiple_of(t * CHUNK, CHUNK), CHUNK)]
        return pltpu.make_async_copy(src, down_buf.at[slot], down_sem.at[slot])

    small = [
        pltpu.make_async_copy(src, dst, in_sem.at[i])
        for i, (src, dst) in enumerate(
            [
                (queries, q_in),
                (keys, k_in),
                (fresh_keys, fk_in),
                (values, v_in),
                (fresh_values, fv_in),
                (resid, r_in),
                (gain, g_in),
            ]
        )
    ]
    for copy in small:
        copy.start()

    barrier = pltpu.get_barrier_semaphore()
    pl.semaphore_signal(barrier, inc=1, device_id={"wide": pair}, device_id_type=MESH)

    @pl.loop(1, chips)
    def _(d):
        pl.semaphore_signal(
            barrier,
            inc=1,
            device_id={"wide": 2 * lax.rem(chip + d, chips) + core},
            device_id_type=MESH,
        )

    @pl.loop(0, gu_slots)
    def _(t):
        gate_copy(t).start()
        up_copy(t).start()

    gate_acc[...] = jnp.zeros_like(gate_acc)
    up_acc[...] = jnp.zeros_like(up_acc)

    for copy in small:
        copy.wait()
    scale = 1.0 / math.sqrt(HEAD_SIZE)
    q32 = q_in[...].astype(jnp.float32)
    for r in range(rows):
        for h in range(heads):
            q_heads[r * heads + h : r * heads + h + 1, :] = q32[
                r : r + 1, h * HEAD_SIZE : (h + 1) * HEAD_SIZE
            ]
    position = lax.broadcasted_iota(jnp.int32, (per_kv, length), 1)
    fk32 = fk_in[...].astype(jnp.float32)
    fv32 = fv_in[...].astype(jnp.float32)
    for r in range(rows):
        inside = position < lengths[r]
        for k in range(kv_heads):
            lanes = slice(k * HEAD_SIZE, (k + 1) * HEAD_SIZE)
            first = r * heads + k * per_kv
            q = q_heads[first : first + per_kv, :]
            own_score = jnp.sum(q * fk32[r : r + 1, lanes], axis=-1, keepdims=True) * scale
            scores = (
                lax.dot_general(
                    q.astype(jnp.bfloat16),
                    k_in[r, :, lanes],
                    (((1,), (1,)), ((), ())),
                    preferred_element_type=jnp.float32,
                )
                * scale
            )
            scores = jnp.where(inside, scores, NEG_FILL)
            row_max = jnp.maximum(jnp.max(scores, axis=-1, keepdims=True), own_score)
            weights = jnp.where(inside, jnp.exp(scores - row_max), 0.0)
            own_weight = jnp.exp(own_score - row_max)
            totals = jnp.sum(weights, axis=-1, keepdims=True) + own_weight
            own_low = own_weight.astype(jnp.bfloat16).astype(jnp.float32)
            attended = jnp.dot(
                weights.astype(jnp.bfloat16),
                v_in[r, :, lanes],
                preferred_element_type=jnp.float32,
            )
            attended = (attended + own_low * fv32[r : r + 1, lanes]) / totals
            for i in range(per_kv):
                col = (k * per_kv + i) * HEAD_SIZE
                stream[r : r + 1, col : col + HEAD_SIZE] = attended[i : i + 1, :]

    total = stream[...] + r_in[...].astype(jnp.float32)
    stream[...] = total
    mean = jnp.sum(total * total, axis=-1, keepdims=True) * (1.0 / width)
    normed = (total * lax.rsqrt(mean + 1e-05) * g_in[...].astype(jnp.float32)).astype(jnp.bfloat16)

    my_slot = core * chips + chip
    piece = width // gather_pieces
    for q in range(gather_pieces):
        gathered[q, my_slot] = normed[:, q * piece : (q + 1) * piece]

    def ag_copy(q, d):
        return pltpu.make_async_remote_copy(
            gathered.at[q, my_slot],
            gathered.at[q, my_slot],
            ag_send.at[q, d],
            ag_recv.at[q, d],
            device_id={"wide": 2 * lax.rem(chip + d, chips) + core},
            device_id_type=MESH,
        )

    def fw_copy(q, d):
        slot = core * chips + lax.rem(chip - d + chips, chips)
        return pltpu.make_async_remote_copy(
            gathered.at[q, slot],
            gathered.at[q, slot],
            fw_send.at[q, d],
            fw_recv.at[q, d],
            device_id={"wide": pair},
            device_id_type=MESH,
        )

    pl.semaphore_wait(barrier, chips)

    @pl.loop(0, gather_pieces)
    def _(q):
        fw_copy(q, 0).start()

        @pl.loop(1, chips)
        def _(d):
            ag_copy(q, d).start()

    def forward(q):
        @pl.loop(1, chips)
        def _(d):
            ag_copy(q, d).wait_recv()
            fw_copy(q, d).start()

    forward(0)

    @pl.loop(0, chunks)
    def _(t):
        q = t // per_gather
        j = lax.rem(t, per_gather)

        @pl.when(j == 0)
        def _():
            @pl.loop(0, chips)
            def _(d):
                fw_copy(q, d).wait_recv()

        @pl.when(jnp.logical_and(j == min(1, per_gather - 1), q + 1 < gather_pieces))
        def _():
            forward(q + 1)

        cols = pl.ds(pl.multiple_of(j * CHUNK, CHUNK), CHUNK)
        x = gathered[q, :, :, cols].reshape(rows * n, CHUNK)
        slot = lax.rem(t, gu_slots)
        gate_copy(t).wait()
        gate_acc[...] += jnp.dot(x, gate_buf[slot], preferred_element_type=jnp.float32)
        up_copy(t).wait()
        up_acc[...] += jnp.dot(x, up_buf[slot], preferred_element_type=jnp.float32)

        @pl.when(t + gu_slots < chunks)
        def _():
            gate_copy(t + gu_slots).start()
            up_copy(t + gu_slots).start()

        later = 2 * (t + gu_slots - chunks)

        @pl.when(jnp.logical_and(later >= 0, later < dn_slots))
        def _():
            down_copy(later).start()
            down_copy(later + 1).start()

    gate = gate_acc[...]
    hidden[...] = (gate / (1.0 + jnp.exp(-gate)) * up_acc[...]).astype(jnp.bfloat16)

    mine = pl.multiple_of(core * half, half)
    other = pl.multiple_of((1 - core) * half, half)

    def pair_copy(p):
        return pltpu.make_async_remote_copy(
            part16.at[p, pl.ds(other, half)],
            from_pair.at[p],
            pair_send.at[p],
            pair_recv.at[p],
            device_id={"wide": pair},
            device_id_type=MESH,
        )

    def rs_copy(p, d):
        dest = lax.rem(chip + d, chips)
        return pltpu.make_async_remote_copy(
            to_chips.at[p, dest],
            from_chips.at[p, chip],
            rs_send.at[p, d],
            rs_recv.at[p, d],
            device_id={"wide": 2 * dest + core},
            device_id_type=MESH,
        )

    def reduce_pair(p):
        pair_copy(p).wait_recv()
        both = part32[p, pl.ds(mine, half)] + from_pair[p].astype(jnp.float32)
        to_chips[p] = both.astype(jnp.bfloat16).reshape(to_chips.shape[1:])

        @pl.loop(1, chips)
        def _(d):
            rs_copy(p, d).start()

        from_chips[p, chip] = to_chips[p, chip]

    @pl.loop(0, chunks)
    def _(t):
        p = t // per_sum
        j = lax.rem(t, per_sum)
        cols = pl.ds(pl.multiple_of(j * CHUNK, CHUNK), CHUNK)
        down_copy(t).wait()
        part = jnp.dot(
            hidden[...], down_buf[lax.rem(t, dn_slots)], preferred_element_type=jnp.float32
        )
        part32[p, :, cols] = part
        part16[p, :, cols] = part.astype(jnp.bfloat16)

        @pl.when(t + dn_slots < chunks)
        def _():
            down_copy(t + dn_slots).start()

        @pl.when(j == per_sum - 1)
        def _():
            pair_copy(p).start()

        @pl.when(jnp.logical_and(j == min(1, per_sum - 1), p > 0))
        def _():
            reduce_pair(p - 1)

    reduce_pair(sum_pieces - 1)

    columns = width // sum_pieces
    for p in range(sum_pieces):

        @pl.loop(1, chips)
        def _(d):
            rs_copy(p, d).wait_recv()

        span = slice(p * columns, (p + 1) * columns)
        summed = jnp.sum(from_chips[p].astype(jnp.float32), axis=0)
        out[:, span] = (stream[:, span] + summed).astype(out.dtype)

    @pl.loop(0, gather_pieces)
    def _(q):
        fw_copy(q, 0).wait_send()

        @pl.loop(1, chips)
        def _(d):
            ag_copy(q, d).wait_send()
            fw_copy(q, d).wait_send()

    @pl.loop(0, sum_pieces)
    def _(p):
        pair_copy(p).wait_send()

        @pl.loop(1, chips)
        def _(d):
            rs_copy(p, d).wait_send()


def body(
    queries,
    key_cache_array,
    value_cache_array,
    fresh_keys,
    fresh_values,
    lengths,
    resid,
    gain,
    gate_weight,
    up_weight,
    down_weight,
    *,
    n,
):
    rows, width = queries.shape
    units = gate_weight.shape[1]
    chips = n // 2
    heads = width // HEAD_SIZE
    chunks = width // CHUNK
    gu_slots = min(12, chunks)
    dn_slots = min(8, chunks)
    gq, sp = GATHER_PIECES, SUM_PIECES
    bf, f32 = jnp.bfloat16, jnp.float32
    any_spec = pl.BlockSpec(memory_space=pl.ANY)
    weights_bytes = 2 * 3 * width * units
    return pl.pallas_call(
        functools.partial(kernel, n, gq, sp),
        out_shape=jax.ShapeDtypeStruct((rows, width), bf),
        in_specs=[pl.BlockSpec(memory_space=pltpu.SMEM)] + [any_spec] * 10,
        out_specs=pl.BlockSpec(memory_space=pltpu.VMEM),
        scratch_shapes=[
            pltpu.VMEM(queries.shape, bf),
            pltpu.VMEM(key_cache_array.shape, bf),
            pltpu.VMEM(value_cache_array.shape, bf),
            pltpu.VMEM(fresh_keys.shape, bf),
            pltpu.VMEM(fresh_values.shape, bf),
            pltpu.VMEM(resid.shape, bf),
            pltpu.VMEM((1, width), bf),
            pltpu.VMEM((rows * heads, HEAD_SIZE), f32),
            pltpu.VMEM((rows, width), f32),
            pltpu.VMEM((gu_slots, CHUNK, units), bf),
            pltpu.VMEM((gu_slots, CHUNK, units), bf),
            pltpu.VMEM((dn_slots, units, CHUNK), bf),
            pltpu.VMEM((gq, n, rows, width // gq), bf),
            pltpu.VMEM((n * rows, units), f32),
            pltpu.VMEM((n * rows, units), f32),
            pltpu.VMEM((n * rows, units), bf),
            pltpu.VMEM((sp, n * rows, width // sp), f32),
            pltpu.VMEM((sp, n * rows, width // sp), bf),
            pltpu.VMEM((sp, chips * rows, width // sp), bf),
            pltpu.VMEM((sp, chips, rows, width // sp), bf),
            pltpu.VMEM((sp, chips, rows, width // sp), bf),
            pltpu.SemaphoreType.DMA((7,)),
            pltpu.SemaphoreType.DMA((gu_slots,)),
            pltpu.SemaphoreType.DMA((gu_slots,)),
            pltpu.SemaphoreType.DMA((dn_slots,)),
            pltpu.SemaphoreType.DMA((gq, chips)),
            pltpu.SemaphoreType.DMA((gq, chips)),
            pltpu.SemaphoreType.DMA((gq, chips)),
            pltpu.SemaphoreType.DMA((gq, chips)),
            pltpu.SemaphoreType.DMA((sp,)),
            pltpu.SemaphoreType.DMA((sp,)),
            pltpu.SemaphoreType.DMA((sp, chips)),
            pltpu.SemaphoreType.DMA((sp, chips)),
        ],
        compiler_params=pltpu.CompilerParams(
            collective_id=0, has_side_effects=True, vmem_limit_bytes=60 * MIB
        ),
        cost_estimate=pl.CostEstimate(
            flops=2 * n * rows * weights_bytes // 2,
            bytes_accessed=weights_bytes,
            transcendentals=n * rows * units,
        ),
        name="decode_layer",
    )(
        lengths,
        queries,
        key_cache_array,
        value_cache_array,
        fresh_keys,
        fresh_values,
        resid,
        gain.reshape(1, width),
        gate_weight,
        up_weight,
        down_weight,
    )


def solution(mesh):
    rows = P(("groups", "wide"), None)
    cache = P(("groups", "wide"), None, None)
    return jax.shard_map(
        functools.partial(body, n=mesh.shape["wide"]),
        mesh=mesh,
        in_specs=(
            rows,
            cache,
            cache,
            rows,
            rows,
            P(("groups", "wide")),
            rows,
            P(),
            P(None, "wide"),
            P(None, "wide"),
            P("wide", None),
        ),
        out_specs=rows,
        check_vma=False,
    )
```

```python
import functools
import math

import jax
import jax.numpy as jnp
from jax import lax
from jax.experimental import pallas as pl
from jax.experimental.pallas import tpu as pltpu
from jax.sharding import PartitionSpec as P

HEAD_SIZE = 128
NEG_FILL = -1e30
MESH = pl.DeviceIdType.MESH
MIB = 1024 * 1024

CHUNK = 512
GATHER_PIECES = 4
SUM_PIECES = 4


def kernel(
    n,
    groups,
    gather_pieces,
    sum_pieces,
    lengths,
    queries,
    keys,
    values,
    fresh_keys,
    fresh_values,
    resid,
    gain,
    gate_w,
    up_w,
    down_w,
    out,
    q_in,
    k_in,
    v_in,
    fk_in,
    fv_in,
    r_in,
    g_in,
    q_heads,
    stream,
    gate_buf,
    up_buf,
    down_buf,
    gathered,
    gate_acc,
    up_acc,
    hidden,
    part32,
    part16,
    from_pair,
    from_x,
    to_chips,
    from_chips,
    in_sem,
    gate_sem,
    up_sem,
    down_sem,
    ag_send,
    ag_recv,
    fw_send,
    fw_recv,
    x_send,
    x_recv,
    fx_send,
    fx_recv,
    pair_send,
    pair_recv,
    px_send,
    px_recv,
    rs_send,
    rs_recv,
):
    rows, width = queries.shape
    heads = width // HEAD_SIZE
    kv_heads = keys.shape[2] // HEAD_SIZE
    per_kv = heads // kv_heads
    length = keys.shape[1]
    chips = n // 2
    chunks = width // CHUNK
    window = gate_buf.shape[2]
    units = gate_w.shape[1]
    per_gather = chunks // gather_pieces
    per_sum = chunks // sum_pieces
    group_rows = rows * chips
    half = groups * group_rows

    group = lax.axis_index("groups")
    me = lax.axis_index("wide")
    chip = me // 2
    core = lax.rem(me, 2)
    pair = me + 1 - 2 * core
    if units == window:
        rows_from, cols_from = pl.ds(0, units), pl.ds(0, units)
    else:
        start = pl.multiple_of(group * (units - window), 128)
        rows_from = cols_from = pl.ds(start, window)

    def gate_copy(t):
        src = gate_w.at[pl.ds(pl.multiple_of(t * CHUNK, CHUNK), CHUNK), cols_from]
        return pltpu.make_async_copy(src, gate_buf.at[t], gate_sem.at[t])

    def up_copy(t):
        src = up_w.at[pl.ds(pl.multiple_of(t * CHUNK, CHUNK), CHUNK), cols_from]
        return pltpu.make_async_copy(src, up_buf.at[t], up_sem.at[t])

    def down_copy(t):
        src = down_w.at[rows_from, pl.ds(pl.multiple_of(t * CHUNK, CHUNK), CHUNK)]
        return pltpu.make_async_copy(src, down_buf.at[t], down_sem.at[t])

    small = [
        pltpu.make_async_copy(src, dst, in_sem.at[i])
        for i, (src, dst) in enumerate(
            [
                (queries, q_in),
                (keys, k_in),
                (fresh_keys, fk_in),
                (values, v_in),
                (fresh_values, fv_in),
                (resid, r_in),
                (gain, g_in),
            ]
        )
    ]
    for copy in small:
        copy.start()

    barrier = pltpu.get_barrier_semaphore()
    pl.semaphore_signal(barrier, inc=1, device_id={"wide": pair}, device_id_type=MESH)
    pl.semaphore_signal(
        barrier, inc=1, device_id={"groups": 1 - group}, device_id_type=MESH
    )

    @pl.loop(1, chips, unroll=chips <= 8)
    def _(d):
        pl.semaphore_signal(
            barrier,
            inc=1,
            device_id={"wide": 2 * lax.rem(chip + d, chips) + core},
            device_id_type=MESH,
        )

    @pl.loop(0, chunks)
    def _(t):
        gate_copy(t).start()
        up_copy(t).start()

    @pl.loop(0, chunks)
    def _(t):
        down_copy(t).start()

    gate_acc[...] = jnp.zeros_like(gate_acc)
    up_acc[...] = jnp.zeros_like(up_acc)

    for copy in small:
        copy.wait()
    scale = 1.0 / math.sqrt(HEAD_SIZE)
    q32 = q_in[...].astype(jnp.float32)
    for r in range(rows):
        for h in range(heads):
            q_heads[r * heads + h : r * heads + h + 1, :] = q32[
                r : r + 1, h * HEAD_SIZE : (h + 1) * HEAD_SIZE
            ]
    position = lax.broadcasted_iota(jnp.int32, (per_kv, length), 1)
    fk32 = fk_in[...].astype(jnp.float32)
    fv32 = fv_in[...].astype(jnp.float32)
    for r in range(rows):
        inside = position < lengths[r]
        for k in range(kv_heads):
            lanes = slice(k * HEAD_SIZE, (k + 1) * HEAD_SIZE)
            first = r * heads + k * per_kv
            q = q_heads[first : first + per_kv, :]
            own_score = jnp.sum(q * fk32[r : r + 1, lanes], axis=-1, keepdims=True) * scale
            scores = (
                lax.dot_general(
                    q.astype(jnp.bfloat16),
                    k_in[r, :, lanes],
                    (((1,), (1,)), ((), ())),
                    preferred_element_type=jnp.float32,
                )
                * scale
            )
            scores = jnp.where(inside, scores, NEG_FILL)
            row_max = jnp.maximum(jnp.max(scores, axis=-1, keepdims=True), own_score)
            weights = jnp.where(inside, jnp.exp(scores - row_max), 0.0)
            own_weight = jnp.exp(own_score - row_max)
            totals = jnp.sum(weights, axis=-1, keepdims=True) + own_weight
            own_low = own_weight.astype(jnp.bfloat16).astype(jnp.float32)
            attended = jnp.dot(
                weights.astype(jnp.bfloat16),
                v_in[r, :, lanes],
                preferred_element_type=jnp.float32,
            )
            attended = (attended + own_low * fv32[r : r + 1, lanes]) / totals
            for i in range(per_kv):
                col = (k * per_kv + i) * HEAD_SIZE
                stream[r : r + 1, col : col + HEAD_SIZE] = attended[i : i + 1, :]

    total = stream[...] + r_in[...].astype(jnp.float32)
    stream[...] = total
    mean = jnp.sum(total * total, axis=-1, keepdims=True) * (1.0 / width)
    normed = (total * lax.rsqrt(mean + 1e-05) * g_in[...].astype(jnp.float32).reshape(1, width)).astype(jnp.bfloat16)

    own_slots = (core * groups + group) * chips
    x_slots = (core * groups + 1 - group) * chips
    piece = width // gather_pieces
    for q in range(gather_pieces):
        gathered[q, own_slots + chip] = normed[:, q * piece : (q + 1) * piece]

    def send(q, slot, send_sem, recv_sem, device):
        return pltpu.make_async_remote_copy(
            gathered.at[q, slot],
            gathered.at[q, slot],
            send_sem,
            recv_sem,
            device_id=device,
            device_id_type=MESH,
        )

    def ag_copy(q, d):
        device = {"wide": 2 * lax.rem(chip + d, chips) + core}
        return send(q, own_slots + chip, ag_send.at[q, d], ag_recv.at[q, d], device)

    def x_copy(q):
        return send(
            q, pl.ds(own_slots, chips), x_send.at[q], x_recv.at[q], {"groups": 1 - group}
        )

    def fw_copy(q):
        return send(q, pl.ds(own_slots, chips), fw_send.at[q], fw_recv.at[q], {"wide": pair})

    def fx_copy(q):
        return send(q, pl.ds(x_slots, chips), fx_send.at[q], fx_recv.at[q], {"wide": pair})

    pl.semaphore_wait(barrier, chips + 1)

    @pl.loop(0, gather_pieces)
    def _(q):
        @pl.loop(1, chips, unroll=chips <= 8)
        def _(d):
            ag_copy(q, d).start()

    def forward(q):
        @pl.loop(1, chips, unroll=chips <= 8)
        def _(d):
            ag_copy(q, d).wait_recv()

        x_copy(q).start()
        fw_copy(q).start()

    def forward_x(q):
        x_copy(q).wait_recv()
        fx_copy(q).start()

    forward(0)
    if gather_pieces > 1:
        forward(1)
    forward_x(0)
    if gather_pieces > 2:
        forward(2)

    @pl.loop(0, chunks, unroll=4)
    def _(t):
        q = t // per_gather
        j = lax.rem(t, per_gather)

        @pl.when(j == 0)
        def _():
            fw_copy(q).wait_recv()
            fx_copy(q).wait_recv()

        @pl.when(jnp.logical_and(j == per_gather // 2, q + 1 < gather_pieces))
        def _():
            forward_x(q + 1)

            @pl.when(q + 3 < gather_pieces)
            def _():
                forward(q + 3)

        cols = pl.ds(pl.multiple_of(j * CHUNK, CHUNK), CHUNK)
        x = gathered[q, :, :, cols].reshape(rows * n * groups, CHUNK)
        gate_copy(t).wait()
        gate_acc[...] += jnp.dot(x, gate_buf[t], preferred_element_type=jnp.float32)
        up_copy(t).wait()
        up_acc[...] += jnp.dot(x, up_buf[t], preferred_element_type=jnp.float32)

    gate = gate_acc[...]
    unit = lax.broadcasted_iota(jnp.int32, gate.shape, 1) + group * (units - window)
    act = jnp.where(unit >= group * window, gate / (1.0 + jnp.exp(-gate)) * up_acc[...], 0.0)
    hidden[...] = act.astype(jnp.bfloat16)

    mine = pl.multiple_of(core * half, half)
    other = pl.multiple_of((1 - core) * half, half)
    own_rows = pl.ds(pl.multiple_of(mine + group * group_rows, group_rows), group_rows)
    x_rows = pl.ds(pl.multiple_of(mine + (1 - group) * group_rows, group_rows), group_rows)

    def pair_copy(p):
        return pltpu.make_async_remote_copy(
            part16.at[p, pl.ds(other, half)],
            from_pair.at[p],
            pair_send.at[p],
            pair_recv.at[p],
            device_id={"wide": pair},
            device_id_type=MESH,
        )

    def px_copy(p):
        return pltpu.make_async_remote_copy(
            part16.at[p, x_rows],
            from_x.at[p],
            px_send.at[p],
            px_recv.at[p],
            device_id={"groups": 1 - group},
            device_id_type=MESH,
        )

    def rs_copy(p, d):
        dest = lax.rem(chip + d, chips)
        return pltpu.make_async_remote_copy(
            to_chips.at[p, dest],
            from_chips.at[p, chip],
            rs_send.at[p, d],
            rs_recv.at[p, d],
            device_id={"wide": 2 * dest + core},
            device_id_type=MESH,
        )

    def reduce_pair(p):
        pair_copy(p).wait_recv()
        here = pl.ds(pl.multiple_of((1 - group) * group_rows, group_rows), group_rows)
        both = part32[p, x_rows] + from_pair[p, here].astype(jnp.float32)
        part16[p, x_rows] = both.astype(jnp.bfloat16)
        px_copy(p).start()
        here = pl.ds(pl.multiple_of(group * group_rows, group_rows), group_rows)
        part32[p, own_rows] += from_pair[p, here].astype(jnp.float32)

    def reduce_groups(p):
        px_copy(p).wait_recv()
        both = part32[p, own_rows] + from_x[p].astype(jnp.float32)
        to_chips[p] = both.astype(jnp.bfloat16).reshape(to_chips.shape[1:])

        @pl.loop(1, chips, unroll=chips <= 8)
        def _(d):
            rs_copy(p, d).start()

        from_chips[p, chip] = to_chips[p, chip]

    @pl.loop(0, chunks, unroll=4)
    def _(t):
        p = t // per_sum
        j = lax.rem(t, per_sum)
        cols = pl.ds(pl.multiple_of(j * CHUNK, CHUNK), CHUNK)
        down_copy(t).wait()
        part = jnp.dot(hidden[...], down_buf[t], preferred_element_type=jnp.float32)
        part32[p, :, cols] = part
        part16[p, :, cols] = part.astype(jnp.bfloat16)

        @pl.when(j == per_sum - 1)
        def _():
            pair_copy(p).start()

            @pl.when(p >= 1)
            def _():
                reduce_pair(p - 1)

    reduce_pair(sum_pieces - 1)

    @pl.loop(0, sum_pieces, unroll=True)
    def _(p):
        reduce_groups(p)

    columns = width // sum_pieces
    for p in range(sum_pieces):

        @pl.loop(1, chips, unroll=chips <= 8)
        def _(d):
            rs_copy(p, d).wait_recv()

        span = slice(p * columns, (p + 1) * columns)
        summed = jnp.sum(from_chips[p].astype(jnp.float32), axis=0)
        out[:, span] = (stream[:, span] + summed).astype(out.dtype)

    @pl.loop(0, gather_pieces)
    def _(q):
        x_copy(q).wait_send()
        fw_copy(q).wait_send()
        fx_copy(q).wait_send()

        @pl.loop(1, chips, unroll=chips <= 8)
        def _(d):
            ag_copy(q, d).wait_send()

    @pl.loop(0, sum_pieces, unroll=True)
    def _(p):
        pair_copy(p).wait_send()
        px_copy(p).wait_send()

        @pl.loop(1, chips, unroll=chips <= 8)
        def _(d):
            rs_copy(p, d).wait_send()


def body(
    queries,
    key_cache_array,
    value_cache_array,
    fresh_keys,
    fresh_values,
    lengths,
    resid,
    gain,
    gate_weight,
    up_weight,
    down_weight,
    *,
    n,
    groups,
):
    rows, width = queries.shape
    units = gate_weight.shape[1]
    chips = n // 2
    heads = width // HEAD_SIZE
    chunks = width // CHUNK
    window = units if units % 128 else -(-units // 256) * 128
    all_rows = n * groups * rows
    half = all_rows // 2
    gq, sp = GATHER_PIECES, SUM_PIECES
    bf, f32 = jnp.bfloat16, jnp.float32
    any_spec = pl.BlockSpec(memory_space=pl.ANY)
    weights_bytes = 2 * 3 * width * window
    return pl.pallas_call(
        functools.partial(kernel, n, groups, gq, sp),
        out_shape=jax.ShapeDtypeStruct((rows, width), bf),
        in_specs=[pl.BlockSpec(memory_space=pltpu.SMEM)] + [any_spec] * 10,
        out_specs=pl.BlockSpec(memory_space=pltpu.VMEM),
        scratch_shapes=[
            pltpu.VMEM(queries.shape, bf),
            pltpu.VMEM(key_cache_array.shape, bf),
            pltpu.VMEM(value_cache_array.shape, bf),
            pltpu.VMEM(fresh_keys.shape, bf),
            pltpu.VMEM(fresh_values.shape, bf),
            pltpu.VMEM(resid.shape, bf),
            pltpu.VMEM((width,), bf),
            pltpu.VMEM((rows * heads, HEAD_SIZE), f32),
            pltpu.VMEM((rows, width), f32),
            pltpu.VMEM((chunks, CHUNK, window), bf),
            pltpu.VMEM((chunks, CHUNK, window), bf),
            pltpu.VMEM((chunks, window, CHUNK), bf),
            pltpu.VMEM((gq, n * groups, rows, width // gq), bf),
            pltpu.VMEM((all_rows, window), f32),
            pltpu.VMEM((all_rows, window), f32),
            pltpu.VMEM((all_rows, window), bf),
            pltpu.VMEM((sp, all_rows, width // sp), f32),
            pltpu.VMEM((sp, all_rows, width // sp), bf),
            pltpu.VMEM((sp, half, width // sp), bf),
            pltpu.VMEM((sp, half // groups, width // sp), bf),
            pltpu.VMEM((sp, chips, rows, width // sp), bf),
            pltpu.VMEM((sp, chips, rows, width // sp), bf),
            pltpu.SemaphoreType.DMA((7,)),
            pltpu.SemaphoreType.DMA((chunks,)),
            pltpu.SemaphoreType.DMA((chunks,)),
            pltpu.SemaphoreType.DMA((chunks,)),
        ]
        + [pltpu.SemaphoreType.DMA((gq, chips))] * 2
        + [pltpu.SemaphoreType.DMA((gq,))] * 6
        + [pltpu.SemaphoreType.DMA((sp,))] * 4
        + [pltpu.SemaphoreType.DMA((sp, chips))] * 2,
        compiler_params=pltpu.CompilerParams(
            collective_id=0, has_side_effects=True, vmem_limit_bytes=60 * MIB
        ),
        cost_estimate=pl.CostEstimate(
            flops=all_rows * weights_bytes,
            bytes_accessed=weights_bytes,
            transcendentals=all_rows * window,
        ),
        name="decode_layer",
    )(
        lengths,
        queries,
        key_cache_array,
        value_cache_array,
        fresh_keys,
        fresh_values,
        resid,
        gain,
        gate_weight,
        up_weight,
        down_weight,
    )


def solution(mesh):
    rows = P(("groups", "wide"), None)
    cache = P(("groups", "wide"), None, None)
    return jax.shard_map(
        functools.partial(body, n=mesh.shape["wide"], groups=mesh.shape["groups"]),
        mesh=mesh,
        in_specs=(
            rows,
            cache,
            cache,
            rows,
            rows,
            P(("groups", "wide")),
            rows,
            P(),
            P(None, "wide"),
            P(None, "wide"),
            P("wide", None),
        ),
        out_specs=rows,
        check_vma=False,
    )
```

```python
import functools
import math

import jax
import jax.numpy as jnp
from jax import lax
from jax.experimental import pallas as pl
from jax.experimental.pallas import tpu as pltpu
from jax.sharding import PartitionSpec as P

HEAD_SIZE = 128
NEG_FILL = -1e30
MESH = pl.DeviceIdType.MESH
MIB = 1024 * 1024

CHUNK = 512
GATHER_PIECES = 4
SUM_PIECES = 4


def kernel(
    n,
    gather_pieces,
    sum_pieces,
    lengths,
    queries,
    keys,
    values,
    fresh_keys,
    fresh_values,
    resid,
    gain,
    gate_w,
    up_w,
    down_w,
    out,
    q_in,
    k_in,
    v_in,
    fk_in,
    fv_in,
    r_in,
    g_in,
    q_heads,
    stream,
    gate_buf,
    up_buf,
    down_buf,
    gathered,
    gate_acc,
    up_acc,
    hidden,
    part32,
    part16,
    from_pair,
    to_chips,
    from_chips,
    in_sem,
    gate_sem,
    up_sem,
    down_sem,
    ag_send,
    ag_recv,
    fw_send,
    fw_recv,
    pair_send,
    pair_recv,
    rs_send,
    rs_recv,
):
    rows, width = queries.shape
    heads = width // HEAD_SIZE
    kv_heads = keys.shape[2] // HEAD_SIZE
    per_kv = heads // kv_heads
    length = keys.shape[1]
    chips = n // 2
    chunks = width // CHUNK
    gu_slots = gate_buf.shape[0]
    dn_slots = down_buf.shape[0]
    per_gather = chunks // gather_pieces
    per_sum = chunks // sum_pieces
    half = rows * chips

    me = lax.axis_index("wide")
    chip = me // 2
    core = lax.rem(me, 2)
    pair = me + 1 - 2 * core

    def gate_copy(t):
        slot = lax.rem(t, gu_slots)
        src = gate_w.at[pl.ds(pl.multiple_of(t * CHUNK, CHUNK), CHUNK)]
        return pltpu.make_async_copy(src, gate_buf.at[slot], gate_sem.at[slot])

    def up_copy(t):
        slot = lax.rem(t, gu_slots)
        src = up_w.at[pl.ds(pl.multiple_of(t * CHUNK, CHUNK), CHUNK)]
        return pltpu.make_async_copy(src, up_buf.at[slot], up_sem.at[slot])

    def down_copy(t):
        slot = lax.rem(t, dn_slots)
        src = down_w.at[:, pl.ds(pl.multiple_of(t * CHUNK, CHUNK), CHUNK)]
        return pltpu.make_async_copy(src, down_buf.at[slot], down_sem.at[slot])

    small = [
        pltpu.make_async_copy(src, dst, in_sem.at[i])
        for i, (src, dst) in enumerate(
            [
                (queries, q_in),
                (keys, k_in),
                (fresh_keys, fk_in),
                (values, v_in),
                (fresh_values, fv_in),
                (resid, r_in),
                (gain, g_in),
            ]
        )
    ]
    for copy in small:
        copy.start()

    barrier = pltpu.get_barrier_semaphore()
    pl.semaphore_signal(barrier, inc=1, device_id={"wide": pair}, device_id_type=MESH)

    @pl.loop(1, chips, unroll=chips <= 8)
    def _(d):
        pl.semaphore_signal(
            barrier,
            inc=1,
            device_id={"wide": 2 * lax.rem(chip + d, chips) + core},
            device_id_type=MESH,
        )

    @pl.loop(0, gu_slots)
    def _(t):
        gate_copy(t).start()
        up_copy(t).start()

    gate_acc[...] = jnp.zeros_like(gate_acc)
    up_acc[...] = jnp.zeros_like(up_acc)

    for copy in small:
        copy.wait()
    scale = 1.0 / math.sqrt(HEAD_SIZE)
    q32 = q_in[...].astype(jnp.float32)
    for r in range(rows):
        for h in range(heads):
            q_heads[r * heads + h : r * heads + h + 1, :] = q32[
                r : r + 1, h * HEAD_SIZE : (h + 1) * HEAD_SIZE
            ]
    position = lax.broadcasted_iota(jnp.int32, (per_kv, length), 1)
    fk32 = fk_in[...].astype(jnp.float32)
    fv32 = fv_in[...].astype(jnp.float32)
    for r in range(rows):
        inside = position < lengths[r]
        for k in range(kv_heads):
            lanes = slice(k * HEAD_SIZE, (k + 1) * HEAD_SIZE)
            first = r * heads + k * per_kv
            q = q_heads[first : first + per_kv, :]
            own_score = jnp.sum(q * fk32[r : r + 1, lanes], axis=-1, keepdims=True) * scale
            scores = (
                lax.dot_general(
                    q.astype(jnp.bfloat16),
                    k_in[r, :, lanes],
                    (((1,), (1,)), ((), ())),
                    preferred_element_type=jnp.float32,
                )
                * scale
            )
            scores = jnp.where(inside, scores, NEG_FILL)
            row_max = jnp.maximum(jnp.max(scores, axis=-1, keepdims=True), own_score)
            weights = jnp.where(inside, jnp.exp(scores - row_max), 0.0)
            own_weight = jnp.exp(own_score - row_max)
            totals = jnp.sum(weights, axis=-1, keepdims=True) + own_weight
            own_low = own_weight.astype(jnp.bfloat16).astype(jnp.float32)
            attended = jnp.dot(
                weights.astype(jnp.bfloat16),
                v_in[r, :, lanes],
                preferred_element_type=jnp.float32,
            )
            attended = (attended + own_low * fv32[r : r + 1, lanes]) / totals
            for i in range(per_kv):
                col = (k * per_kv + i) * HEAD_SIZE
                stream[r : r + 1, col : col + HEAD_SIZE] = attended[i : i + 1, :]

    total = stream[...] + r_in[...].astype(jnp.float32)
    stream[...] = total
    mean = jnp.sum(total * total, axis=-1, keepdims=True) * (1.0 / width)
    normed = (total * lax.rsqrt(mean + 1e-05) * g_in[...].astype(jnp.float32).reshape(1, width)).astype(jnp.bfloat16)

    my_slot = core * chips + chip
    piece = width // gather_pieces
    for q in range(gather_pieces):
        gathered[q, my_slot] = normed[:, q * piece : (q + 1) * piece]

    def ag_copy(q, d):
        return pltpu.make_async_remote_copy(
            gathered.at[q, my_slot],
            gathered.at[q, my_slot],
            ag_send.at[q, d],
            ag_recv.at[q, d],
            device_id={"wide": 2 * lax.rem(chip + d, chips) + core},
            device_id_type=MESH,
        )

    def fw_copy(q):
        block = gathered.at[q, pl.ds(core * chips, chips)]
        return pltpu.make_async_remote_copy(
            block,
            block,
            fw_send.at[q],
            fw_recv.at[q],
            device_id={"wide": pair},
            device_id_type=MESH,
        )

    pl.semaphore_wait(barrier, chips)

    @pl.loop(0, gather_pieces)
    def _(q):
        @pl.loop(1, chips, unroll=chips <= 8)
        def _(d):
            ag_copy(q, d).start()

    def forward(q):
        @pl.loop(1, chips, unroll=chips <= 8)
        def _(d):
            ag_copy(q, d).wait_recv()

        fw_copy(q).start()

    forward(0)

    @pl.loop(0, chunks, unroll=4)
    def _(t):
        q = t // per_gather
        j = lax.rem(t, per_gather)

        @pl.when(j == 0)
        def _():
            fw_copy(q).wait_recv()

        @pl.when(jnp.logical_and(j == min(1, per_gather - 1), q + 1 < gather_pieces))
        def _():
            forward(q + 1)

        cols = pl.ds(pl.multiple_of(j * CHUNK, CHUNK), CHUNK)
        x = gathered[q, :, :, cols].reshape(rows * n, CHUNK)
        slot = lax.rem(t, gu_slots)
        gate_copy(t).wait()
        gate_acc[...] += jnp.dot(x, gate_buf[slot], preferred_element_type=jnp.float32)
        up_copy(t).wait()
        up_acc[...] += jnp.dot(x, up_buf[slot], preferred_element_type=jnp.float32)

        @pl.when(t + gu_slots < chunks)
        def _():
            gate_copy(t + gu_slots).start()
            up_copy(t + gu_slots).start()

        later = 2 * (t + gu_slots - chunks)

        @pl.when(jnp.logical_and(later >= 0, later < dn_slots))
        def _():
            down_copy(later).start()
            down_copy(later + 1).start()

    gate = gate_acc[...]
    hidden[...] = (gate / (1.0 + jnp.exp(-gate)) * up_acc[...]).astype(jnp.bfloat16)

    mine = pl.multiple_of(core * half, half)
    other = pl.multiple_of((1 - core) * half, half)

    def pair_copy(p):
        return pltpu.make_async_remote_copy(
            part16.at[p, pl.ds(other, half)],
            from_pair.at[p],
            pair_send.at[p],
            pair_recv.at[p],
            device_id={"wide": pair},
            device_id_type=MESH,
        )

    def rs_copy(p, d):
        dest = lax.rem(chip + d, chips)
        return pltpu.make_async_remote_copy(
            to_chips.at[p, dest],
            from_chips.at[p, chip],
            rs_send.at[p, d],
            rs_recv.at[p, d],
            device_id={"wide": 2 * dest + core},
            device_id_type=MESH,
        )

    def reduce_pair(p):
        pair_copy(p).wait_recv()
        both = part32[p, pl.ds(mine, half)] + from_pair[p].astype(jnp.float32)
        to_chips[p] = both.astype(jnp.bfloat16).reshape(to_chips.shape[1:])

        @pl.loop(1, chips, unroll=chips <= 8)
        def _(d):
            rs_copy(p, d).start()

        from_chips[p, chip] = to_chips[p, chip]

    @pl.loop(0, chunks, unroll=4)
    def _(t):
        p = t // per_sum
        j = lax.rem(t, per_sum)
        cols = pl.ds(pl.multiple_of(j * CHUNK, CHUNK), CHUNK)
        down_copy(t).wait()
        part = jnp.dot(
            hidden[...], down_buf[lax.rem(t, dn_slots)], preferred_element_type=jnp.float32
        )
        part32[p, :, cols] = part
        part16[p, :, cols] = part.astype(jnp.bfloat16)

        @pl.when(t + dn_slots < chunks)
        def _():
            down_copy(t + dn_slots).start()

        @pl.when(j == per_sum - 1)
        def _():
            pair_copy(p).start()

        @pl.when(jnp.logical_and(j == min(1, per_sum - 1), p > 0))
        def _():
            reduce_pair(p - 1)

    reduce_pair(sum_pieces - 1)

    columns = width // sum_pieces
    for p in range(sum_pieces):

        @pl.loop(1, chips, unroll=chips <= 8)
        def _(d):
            rs_copy(p, d).wait_recv()

        span = slice(p * columns, (p + 1) * columns)
        summed = jnp.sum(from_chips[p].astype(jnp.float32), axis=0)
        out[:, span] = (stream[:, span] + summed).astype(out.dtype)

    @pl.loop(0, gather_pieces)
    def _(q):
        fw_copy(q).wait_send()

        @pl.loop(1, chips, unroll=chips <= 8)
        def _(d):
            ag_copy(q, d).wait_send()

    @pl.loop(0, sum_pieces)
    def _(p):
        pair_copy(p).wait_send()

        @pl.loop(1, chips, unroll=chips <= 8)
        def _(d):
            rs_copy(p, d).wait_send()


def body(
    queries,
    key_cache_array,
    value_cache_array,
    fresh_keys,
    fresh_values,
    lengths,
    resid,
    gain,
    gate_weight,
    up_weight,
    down_weight,
    *,
    n,
):
    rows, width = queries.shape
    units = gate_weight.shape[1]
    chips = n // 2
    heads = width // HEAD_SIZE
    chunks = width // CHUNK
    gu_slots = min(12, chunks)
    dn_slots = min(8, chunks)
    gq, sp = GATHER_PIECES, SUM_PIECES
    bf, f32 = jnp.bfloat16, jnp.float32
    any_spec = pl.BlockSpec(memory_space=pl.ANY)
    weights_bytes = 2 * 3 * width * units
    return pl.pallas_call(
        functools.partial(kernel, n, gq, sp),
        out_shape=jax.ShapeDtypeStruct((rows, width), bf),
        in_specs=[pl.BlockSpec(memory_space=pltpu.SMEM)] + [any_spec] * 10,
        out_specs=pl.BlockSpec(memory_space=pltpu.VMEM),
        scratch_shapes=[
            pltpu.VMEM(queries.shape, bf),
            pltpu.VMEM(key_cache_array.shape, bf),
            pltpu.VMEM(value_cache_array.shape, bf),
            pltpu.VMEM(fresh_keys.shape, bf),
            pltpu.VMEM(fresh_values.shape, bf),
            pltpu.VMEM(resid.shape, bf),
            pltpu.VMEM((width,), bf),
            pltpu.VMEM((rows * heads, HEAD_SIZE), f32),
            pltpu.VMEM((rows, width), f32),
            pltpu.VMEM((gu_slots, CHUNK, units), bf),
            pltpu.VMEM((gu_slots, CHUNK, units), bf),
            pltpu.VMEM((dn_slots, units, CHUNK), bf),
            pltpu.VMEM((gq, n, rows, width // gq), bf),
            pltpu.VMEM((n * rows, units), f32),
            pltpu.VMEM((n * rows, units), f32),
            pltpu.VMEM((n * rows, units), bf),
            pltpu.VMEM((sp, n * rows, width // sp), f32),
            pltpu.VMEM((sp, n * rows, width // sp), bf),
            pltpu.VMEM((sp, chips * rows, width // sp), bf),
            pltpu.VMEM((sp, chips, rows, width // sp), bf),
            pltpu.VMEM((sp, chips, rows, width // sp), bf),
            pltpu.SemaphoreType.DMA((7,)),
            pltpu.SemaphoreType.DMA((gu_slots,)),
            pltpu.SemaphoreType.DMA((gu_slots,)),
            pltpu.SemaphoreType.DMA((dn_slots,)),
            pltpu.SemaphoreType.DMA((gq, chips)),
            pltpu.SemaphoreType.DMA((gq, chips)),
            pltpu.SemaphoreType.DMA((gq,)),
            pltpu.SemaphoreType.DMA((gq,)),
            pltpu.SemaphoreType.DMA((sp,)),
            pltpu.SemaphoreType.DMA((sp,)),
            pltpu.SemaphoreType.DMA((sp, chips)),
            pltpu.SemaphoreType.DMA((sp, chips)),
        ],
        compiler_params=pltpu.CompilerParams(
            collective_id=0, has_side_effects=True, vmem_limit_bytes=60 * MIB
        ),
        cost_estimate=pl.CostEstimate(
            flops=2 * n * rows * weights_bytes // 2,
            bytes_accessed=weights_bytes,
            transcendentals=n * rows * units,
        ),
        name="decode_layer",
    )(
        lengths,
        queries,
        key_cache_array,
        value_cache_array,
        fresh_keys,
        fresh_values,
        resid,
        gain,
        gate_weight,
        up_weight,
        down_weight,
    )


def solution(mesh):
    rows = P(("groups", "wide"), None)
    cache = P(("groups", "wide"), None, None)
    return jax.shard_map(
        functools.partial(body, n=mesh.shape["wide"]),
        mesh=mesh,
        in_specs=(
            rows,
            cache,
            cache,
            rows,
            rows,
            P(("groups", "wide")),
            rows,
            P(),
            P(None, "wide"),
            P(None, "wide"),
            P("wide", None),
        ),
        out_specs=rows,
        check_vma=False,
    )
```
